32 devices in a mesh: row: 4 (over y, core), col: 8 (over z, x).
Axes of the slice: x: 2, y: 2, z: 4, core: 2. Of those that a mesh axis runs over, the one named last changes fastest.
Arguments:
- slab_points: bfloat16 [64, 4096], P(None, ('row', 'col')), may hold values from -6 to 6
- col_points: bfloat16 [64, 131072], P(None, 'col'), may hold values from -6 to 6
- probes: bfloat16 [64, 131072], P(None, 'col'), may hold values from -6 to 6
Outputs:
- basis: bfloat16 [64, 4096], P(None, ('row', 'col'))
- image: float32 [64, 131072], P(None, ('col', 'row'))
The draws below stay inside these ranges and needn't reach their ends.
All inputs are finite; a program needn't handle non-finite values.
Results may differ from the reference program's by a relative error of at most 0.0052.
Values may be sent and summed in bfloat16 or wider, within the bound.
No kernel may reach another device: no remote copies, remote signals or barrier semaphores. Data moves between devices by JAX's collectives and lax.ppermute only.
A program may use at most 128 MiB of HBM per device.

```python
import math
import jax
import jax.numpy as jnp
from jax import lax

DIM = 64
PROBES = 64
SLAB = 4096
NPTS = 131072


def draw_slab_points(key, part):
    key = jax.random.fold_in(key, 17)
    values = jnp.clip(jax.random.normal(key, (DIM, SLAB), jnp.float32), -6.0, 6.0)
    return values.astype(jnp.bfloat16)


def draw_col_points(key, part):
    key = jax.random.fold_in(key, 29)
    values = jnp.clip(jax.random.normal(key, (DIM, NPTS), jnp.float32), -6.0, 6.0)
    return values.astype(jnp.bfloat16)


def levels(key, extent, cuts, least, top_value):
    def one(position, blocks):
        draws = jax.random.uniform(jax.random.fold_in(jax.random.fold_in(key, 6), position), (blocks,), jnp.float32, least / len(cuts), top_value / len(cuts))
        return jnp.repeat(jnp.exp(draws), extent[position] // blocks).reshape((-1,) + (1,) * (len(extent) - position - 1))

    level = one(*cuts[0])
    for cut in cuts[1:]:
        level = level * one(*cut)
    return level


def bell_draw(rng, shape, scale, limit, shards=(), kind=jnp.bfloat16):
    loudness = levels(rng, shape, shards, -0.22, 0.18) if shards else 1.0
    entries = jax.random.normal(rng, shape, jnp.float32) * scale * loudness
    return jnp.minimum(jnp.maximum(entries, -limit), limit).astype(kind)


def setup_inputs(seed: int = 0) -> dict:
    seeds = jax.random.split(jax.random.key(seed), 4)
    return {
        "slab_points": draw_slab_points(jax.random.fold_in(seeds[3], 71), 0),
        "col_points": draw_col_points(jax.random.fold_in(seeds[3], 71), 0),
        "probes": bell_draw(seeds[2], (PROBES, NPTS), 1.0, 6.0, ((1, 8),)),
    }


def kernel_block(slab_points, slab_norm, col_block, norm_block):
    inner = lax.dot_general(slab_points.astype(jnp.float32), col_block.astype(jnp.float32), (((0,), (0,)), ((), ())), preferred_element_type=jnp.float32)
    distance = slab_norm[:, None] + norm_block[None, :] - 2.0 * inner
    return jnp.exp(-8.0 * distance / DIM).astype(jnp.bfloat16)

def reference(slab_points, col_points, probes):
    slab_norm = lax.optimization_barrier(jnp.sum(slab_points.astype(jnp.float32) ** 2, axis=0))
    col_norm = lax.optimization_barrier(jnp.sum(col_points.astype(jnp.float32) ** 2, axis=0))
    width = math.gcd(NPTS, 4096)
    count = NPTS // width

    def sample_step(total, which):
        start = (which * width).astype(jnp.int32)
        cols = lax.dynamic_slice_in_dim(col_points, start, width, 1)
        norms = lax.dynamic_slice_in_dim(col_norm, start, width, 0)
        kernel = kernel_block(slab_points, slab_norm, cols, norms)
        probe_block = lax.dynamic_slice_in_dim(probes, start, width, 1)
        return (total + lax.dot_general(probe_block.astype(jnp.float32), kernel.astype(jnp.float32), (((1,), (1,)), ((), ())), preferred_element_type=jnp.float32), None)
    sample, unused = lax.scan(sample_step, jnp.zeros((PROBES, SLAB), jnp.float32), jnp.arange(count, dtype=jnp.int32))
    gram = jnp.dot(sample, sample.T, precision=lax.Precision.HIGHEST) / SLAB
    lower = jnp.linalg.cholesky(gram)
    basis = jax.scipy.linalg.solve_triangular(lower, sample, lower=True).astype(jnp.bfloat16)

    def image_step(carry, which):
        start = (which * width).astype(jnp.int32)
        cols = lax.dynamic_slice_in_dim(col_points, start, width, 1)
        norms = lax.dynamic_slice_in_dim(col_norm, start, width, 0)
        kernel = kernel_block(slab_points, slab_norm, cols, norms)
        return (carry, jnp.dot(basis.astype(jnp.float32), kernel.astype(jnp.float32), preferred_element_type=jnp.float32))
    unused_carry, blocks = lax.scan(image_step, jnp.float32(0.0), jnp.arange(count, dtype=jnp.int32))
    image_scale = jnp.sqrt(jnp.float32(PROBES * NPTS) / jnp.trace(gram)) / SLAB
    image = jnp.transpose(blocks, (1, 0, 2)).reshape(PROBES, NPTS) * image_scale
    return (basis, image)
```

```python
import functools

import jax
import jax.numpy as jnp
from jax import lax
from jax.experimental import pallas as pl
from jax.experimental.pallas import tpu as pltpu
from jax.sharding import PartitionSpec as P

MIB = 1024 * 1024


def params(mib):
    return pltpu.CompilerParams(vmem_limit_bytes=mib * MIB)


def split(x, pieces):
    out = []
    for _ in range(pieces):
        piece = x.astype(jnp.bfloat16)
        x = x - piece.astype(jnp.float32)
        out.append(piece)
    return out


def extended(points, scale=None):
    dims, count = points.shape
    wide = points.astype(jnp.float32)
    norm = -0.5 * jnp.sum(wide * wide, axis=0, keepdims=True)
    row = lax.broadcasted_iota(jnp.int32, (128 - dims, count), 0)
    at = 3 if scale is None else 0
    ones = 3 - at
    factor = 1.0 if scale is None else scale
    extra = jnp.where((row >= ones) & (row < ones + 3), factor, 0.0)
    for i, piece in enumerate(split(norm, 3)):
        extra = jnp.where(row == at + i, piece.astype(jnp.float32) * factor, extra)
    if scale is not None:
        points = (wide * scale).astype(jnp.bfloat16)
    return jnp.concatenate([points, extra.astype(jnp.bfloat16)], axis=0)


def chunks_of(*refs):
    return [ref[i] for ref in refs for i in range(ref.shape[0])]


def resident(shape, dtype):
    return pltpu.VMEM(shape, dtype)


def held(x):
    return pltpu.with_memory_space_constraint(x, pltpu.VMEM)


def pinned(x):
    return pltpu.with_memory_space_constraint(x, pltpu.HBM)


WHOLE = pl.BlockSpec(memory_space=pltpu.VMEM)
SCALAR = pl.BlockSpec(memory_space=pltpu.SMEM)


def add_sample(slab_ext, cols, probes, total, kept_ref, first, mine):
    step = min(256, total.shape[1])
    group = 4096
    size = 512
    own = kept_ref.shape[0] - size
    places = []
    for j in range(cols.shape[0] // size):
        place = first + j * size - mine
        place = jnp.where((place >= 0) & (place < own), place, own)
        places.append(pl.ds(pl.multiple_of(place, size), size))
    for i in range(total.shape[1] // step):
        at = slice(i * step, (i + 1) * step)
        slab = slab_ext[:, at]
        for g in range(cols.shape[0] // group):
            kernel = []
            for j in range(g * group // size, (g + 1) * group // size):
                rows = slice(j * size, (j + 1) * size)
                x = jnp.dot(cols[rows, :], slab, preferred_element_type=jnp.float32)
                k = jnp.exp(x).astype(jnp.bfloat16)
                kept_ref[places[j], at] = k
                kernel.append(k)
            total[:, at] += jnp.dot(
                probes[:, g * group : (g + 1) * group],
                jnp.concatenate(kernel, axis=0),
                preferred_element_type=jnp.float32,
            )


def start_sample(chunks, me_ref, slab_ref, slab_ext, total):
    side = me_ref[0] & 1
    points = [slab_ref[2 * k + (side ^ flip)] for k, flip in chunks]
    slab_ext[...] = extended(jnp.concatenate(points, axis=1), scale_of(slab_ref))
    total[...] = jnp.zeros_like(total)


def scale_of(slab_ref):
    return 16.0 / slab_ref.shape[1]


def end_sample(total, out_ref):
    share = out_ref.shape[2]
    for i in range(out_ref.shape[0]):
        out_ref[i] = total[:, i * share : (i + 1) * share]


def first_sample_kernel(chunks, me_ref, slab_ref, cols_ref, probes_ref, out_ref, kept_ref, cols_out,
                        turned_out, probes_out, slab_ext, total):
    step = pl.program_id(0)
    width = cols_ref.shape[1]

    @pl.when(step == 0)
    def _():
        start_sample(chunks, me_ref, slab_ref, slab_ext, total)

    at = pl.ds(pl.multiple_of(step * width, width), width)
    cols = extended(cols_ref[...])
    probes = probes_ref[...]
    turned = cols.T
    cols_out[:, at] = cols
    turned_out[at, :] = turned
    probes_out[:, at] = probes
    mine = me_ref[1] * (kept_ref.shape[0] - 512)
    add_sample(slab_ext, turned, probes, total, kept_ref, step * width, mine)

    @pl.when(step == pl.num_programs(0) - 1)
    def _():
        end_sample(total, out_ref)


def next_sample_kernel(chunks, me_ref, slab_ref, cols_ref, probes_ref, _, out_ref, kept_ref, slab_ext,
                       total):
    start_sample(chunks, me_ref, slab_ref, slab_ext, total)
    width = 8192
    mine = me_ref[1] * (kept_ref.shape[0] - 512)

    @pl.loop(0, cols_ref.shape[0] // width)
    def _(step):
        at = pl.ds(pl.multiple_of(step * width, width), width)
        add_sample(slab_ext, cols_ref[at, :], probes_ref[:, at], total, kept_ref, step * width, mine)

    end_sample(total, out_ref)


def sample_scratch(chunks, share, n):
    count = len(chunks) * share
    return [pltpu.VMEM((128, count), jnp.bfloat16), pltpu.VMEM((n, count), jnp.float32)]


def sample_cost(count, points):
    return pl.CostEstimate(
        flops=4 * 256 * count * points, bytes_accessed=512 * points, transcendentals=count * points
    )


def first_sample_call(chunks, me, slab, cols, probes, own):
    _, dims, share = slab.shape
    n, points = probes.shape
    width = 4096
    return pl.pallas_call(
        functools.partial(first_sample_kernel, chunks),
        grid=(points // width,),
        in_specs=[
            SCALAR,
            WHOLE,
            pl.BlockSpec((dims, width), lambda i: (0, i)),
            pl.BlockSpec((n, width), lambda i: (0, i)),
        ],
        out_specs=[WHOLE] * 5,
        out_shape=[
            jax.ShapeDtypeStruct((len(chunks), n, share), jnp.float32),
            resident((own + 512, len(chunks) * share), jnp.bfloat16),
            resident((128, points), jnp.bfloat16),
            resident((points, 128), jnp.bfloat16),
            resident((n, points), jnp.bfloat16),
        ],
        scratch_shapes=sample_scratch(chunks, share, n),
        compiler_params=params(10),
        cost_estimate=sample_cost(len(chunks) * share, points),
        name="sample_first",
    )(me, slab, pinned(cols), pinned(probes))


def next_sample_call(chunks, me, slab, cols_ext, probes, own, after):
    _, dims, share = slab.shape
    n, points = probes.shape
    return pl.pallas_call(
        functools.partial(next_sample_kernel, chunks),
        in_specs=[SCALAR] + [WHOLE] * 4,
        out_specs=[WHOLE] * 2,
        out_shape=[
            jax.ShapeDtypeStruct((len(chunks), n, share), jnp.float32),
            resident((own + 512, len(chunks) * share), jnp.bfloat16),
        ],
        scratch_shapes=sample_scratch(chunks, share, n),
        compiler_params=params(8),
        cost_estimate=sample_cost(len(chunks) * share, points),
        name="sample_next",
    )(me, slab, held(cols_ext), held(probes), after)


def tile_kernel(chunks, me_ref, slab_ref, cols_ref, out_ref, token_ref, slab_ext):
    token_ref[...] = jnp.zeros_like(token_ref)
    count, wide = out_ref.shape
    side = me_ref[0] & 1
    points = [slab_ref[base + 2 * k + (side ^ flip)] for base, k, flip in chunks]
    slab_ext[...] = extended(jnp.concatenate(points, axis=1), scale_of(slab_ref)).T
    mine = me_ref[1] * wide
    width = min(4096, wide)

    @pl.loop(0, wide // width)
    def _(step):
        for j in range(width // 512):
            to = pl.multiple_of(step * width + j * 512, 512)
            cols = cols_ref[:, pl.ds(pl.multiple_of(mine + to, 512), 512)]
            for i in range(count // 512):
                rows = slice(i * 512, (i + 1) * 512)
                x = jnp.dot(slab_ext[rows, :], cols, preferred_element_type=jnp.float32)
                out_ref[rows, pl.ds(to, 512)] = jnp.exp(x).astype(jnp.bfloat16)


def tile_call(me, slab, chunks, cols_ext, wide):
    dims, share = slab.shape[1:]
    count = len(chunks) * share
    return pl.pallas_call(
        functools.partial(tile_kernel, chunks),
        in_specs=[SCALAR, WHOLE, WHOLE],
        out_specs=[WHOLE, WHOLE],
        out_shape=[
            resident((count, wide), jnp.bfloat16),
            jax.ShapeDtypeStruct((8, 128), jnp.float32),
        ],
        scratch_shapes=[pltpu.VMEM((count, 128), jnp.bfloat16)],
        compiler_params=params(6 + count // 1024),
        cost_estimate=pl.CostEstimate(
            flops=2 * 256 * count * wide,
            bytes_accessed=2 * count * wide,
            transcendentals=count * wide,
        ),
        name="tile",
    )(me, slab, held(cols_ext))


def sum_kernel(a_ref, b_ref, *refs):
    refs[-1][...] = a_ref[...] + b_ref[...]


def sum_call(a, b, *after):
    return pl.pallas_call(
        sum_kernel,
        in_specs=[WHOLE] * (2 + len(after)),
        out_specs=WHOLE,
        out_shape=jax.ShapeDtypeStruct(a.shape, a.dtype),
        compiler_params=params(8),
        name="sum",
    )(a, b, *after)


def later_kernel(x_ref, _, out_ref):
    out_ref[...] = x_ref[...]


def later_call(x, after):
    return pl.pallas_call(
        later_kernel,
        in_specs=[WHOLE] * 2,
        out_specs=WHOLE,
        out_shape=jax.ShapeDtypeStruct(x.shape, x.dtype),
        compiler_params=params(8),
        name="later",
    )(x, after)


def join_kernel(a_ref, b_ref, *refs):
    out_ref = refs[-1]
    half = a_ref.shape[0]
    out_ref[:half] = a_ref[...]
    out_ref[half:] = b_ref[...]


def join_call(a, b, *after):
    return pl.pallas_call(
        join_kernel,
        in_specs=[WHOLE] * (2 + len(after)),
        out_specs=WHOLE,
        out_shape=jax.ShapeDtypeStruct((2 * a.shape[0],) + a.shape[1:], a.dtype),
        compiler_params=params(8),
        name="join",
    )(a, b, *after)


def inverse_factor(gram):
    n = gram.shape[0]
    depth = 4
    high = 8
    shape = (high, 2 * n)
    diagonal = lax.broadcasted_iota(jnp.int32, (n, n), 0) == lax.broadcasted_iota(jnp.int32, (n, n), 1)
    work = jnp.concatenate([gram, jnp.where(diagonal, 1.0, 0.0)], axis=1)
    blocks = [work[i : i + high, :] for i in range(0, n, high)]
    row = lax.broadcasted_iota(jnp.int32, shape, 0)

    def spread(x):
        return jnp.broadcast_to(x, shape)

    for first in range(0, n, depth):
        home, at = divmod(first, high)
        columns = [
            [spread(block[:, first + i : first + i + 1]) for i in range(depth)] for block in blocks[home:]
        ]
        lines = [spread(blocks[home][at + i : at + i + 1, :]) for i in range(depth)]
        entry = {
            (i, j): spread(columns[0][j][at + i : at + i + 1, :])
            for i in range(depth)
            for j in range(i + 1)
        }
        roots = []
        for j in range(depth):
            root = lax.rsqrt(entry[j, j])
            roots.append(root)
            inverse = root * root
            for i in range(j + 1, depth):
                factor = entry[i, j] * inverse
                for k in range(j + 1, i + 1):
                    entry[i, k] = entry[i, k] - factor * entry[k, j]
                lines[i] = lines[i] - factor * lines[j]
                for column in columns:
                    column[i] = column[i] - factor * column[j]
        scaled = [line * root for line, root in zip(lines, roots)]
        for b, column in enumerate(columns):
            block = blocks[home + b]
            update = (column[0] * roots[0]) * scaled[0]
            for i in range(1, depth):
                update = update + (column[i] * roots[i]) * scaled[i]
            if b:
                block = block - update
            else:
                block = jnp.where(row >= at + depth, block - update, block)
                for i in range(depth):
                    block = jnp.where(row == at + i, scaled[i], block)
            blocks[home + b] = block
        yield None
    yield jnp.concatenate(blocks, axis=0)[:, n:]


def sides(ref, turned):
    n, share = ref.shape[1:]
    for i, chunk in enumerate(chunks_of(ref)):
        turned[:, i * share : (i + 1) * share] = jnp.concatenate(split(chunk, 3), axis=0)
    pieces = turned[...]
    whole = lax.dot_general(
        pieces, pieces, (((1,), (1,)), ((), ())), preferred_element_type=jnp.float32
    )
    lines = whole[:n] + whole[n : 2 * n] + whole[2 * n :]
    return lines[:, :n] + lines[:, n : 2 * n] + lines[:, 2 * n :]


def product(turned, tiles, at, n, columns_first=False):
    first = 0
    lines = None
    for tile in tiles:
        last = first + tile.shape[1 if columns_first else 0]
        part = lax.dot_general(
            turned[: 2 * n, first:last],
            tile[at, :] if columns_first else tile[:, at],
            (((1,), (1 if columns_first else 0,)), ((), ())),
            preferred_element_type=jnp.float32,
        )
        lines = part if lines is None else lines + part
        first = last
    return lines[:n] + lines[n:]


def side_scratch(count, n):
    return [pltpu.VMEM((3 * n, count), jnp.bfloat16)]


def partial_kernel(columns_first, sample_ref, *refs):
    *tiles, gram_ref, raw_ref, turned = refs
    n = sample_ref.shape[1]
    gram_ref[...] = sides(sample_ref, turned)
    width = 512
    for i in range(raw_ref.shape[1] // width):
        at = slice(i * width, (i + 1) * width)
        raw_ref[:, at] = product(turned, tiles, at, n, columns_first)


def partial_call(sample, tiles, wide, columns_first=False):
    parts, n, share = sample.shape
    count = parts * share
    return pl.pallas_call(
        functools.partial(partial_kernel, columns_first),
        in_specs=[WHOLE] * (1 + len(tiles)),
        out_specs=[WHOLE, WHOLE],
        out_shape=[
            jax.ShapeDtypeStruct((n, n), jnp.float32),
            jax.ShapeDtypeStruct((n, wide), jnp.float32),
        ],
        scratch_shapes=side_scratch(count, n),
        compiler_params=params(6 + count // 1024),
        cost_estimate=pl.CostEstimate(
            flops=2 * 256 * count * wide, bytes_accessed=2 * count * wide, transcendentals=0
        ),
        name="partial",
    )(sample, *[held(tile) for tile in tiles])


def finish_kernel(total, points, me_ref, sample_ref, near_ref, gram_a, gram_b, raw_a, raw_b, c_ref, d_ref,
                  basis_ref, image_ref, turned, raw, left):
    n = sample_ref.shape[1]
    step = pl.program_id(0)
    half, wide = c_ref.shape

    @pl.when(step == 0)
    def _():
        gram = (sides(sample_ref, turned) + gram_a[...] + gram_b[...]) / total
        rounds = inverse_factor(gram)
        width = wide // 8
        for i in range(8):
            rows = slice(i * width, (i + 1) * width)
            for _ in range(n // 32):
                next(rounds)
            raw[:, rows] = product(turned, (c_ref, d_ref), rows, n) + (raw_a[:, rows] + raw_b[:, rows])
        inverse = next(rounds)
        while inverse is None:
            inverse = next(rounds)
        diagonal = (
            lax.broadcasted_iota(jnp.int32, (n, n), 0) == lax.broadcasted_iota(jnp.int32, (n, n), 1)
        )
        trace = jnp.sum(jnp.where(diagonal, gram, 0.0), keepdims=True)
        scale = jnp.sqrt(float(n * points) / trace) / total
        basis_ref[...] = jnp.dot(
            inverse,
            near_ref[me_ref[0] // 2],
            precision=lax.Precision.HIGHEST,
            preferred_element_type=jnp.float32,
        ).astype(jnp.bfloat16)
        high, low = split(inverse * scale, 2)
        left[...] = jnp.concatenate([high, high, low, low], axis=1)

    @pl.when(step > 0)
    def _():
        width = image_ref.shape[1]
        at = pl.ds(pl.multiple_of((step - 1) * width, width), width)
        pieces = split(raw[:, at], 2)
        image_ref[...] = jnp.dot(
            left[...], jnp.concatenate(pieces + pieces, axis=0), preferred_element_type=jnp.float32
        )


def finish_call(me, sample, near, grams, raws, tiles, total, points):
    _, n, share = sample.shape
    half, wide = tiles[0].shape
    count = 2 * half
    width = wide // 2
    return pl.pallas_call(
        functools.partial(finish_kernel, float(total), float(points)),
        grid=(3,),
        in_specs=[SCALAR] + [WHOLE] * 8,
        out_specs=[
            pl.BlockSpec((n, share), lambda i: (0, 0)),
            pl.BlockSpec((n, width), lambda i: (0, jnp.maximum(i - 1, 0))),
        ],
        out_shape=[
            jax.ShapeDtypeStruct((n, share), jnp.bfloat16),
            jax.ShapeDtypeStruct((n, wide), jnp.float32),
        ],
        scratch_shapes=side_scratch(count, n)
        + [pltpu.VMEM((n, wide), jnp.float32), pltpu.VMEM((n, 4 * n), jnp.bfloat16)],
        compiler_params=params(8 + count // 1024),
        cost_estimate=pl.CostEstimate(
            flops=2 * 256 * count * wide, bytes_accessed=2 * count * wide, transcendentals=0
        ),
        name="finish",
    )(me, sample, near, *grams, *raws, held(tiles[0]), held(tiles[1]))


def exchanged(x, axis, stride):
    return lax.ppermute(x, axis, [(i ^ stride, i) for i in range(lax.axis_size(axis))])


def halvings(size):
    while size > 1:
        size //= 2
        yield size


def body(slab_points, col_points, probes):
    cols = lax.axis_size("col")
    rows = lax.axis_size("row")
    total = slab_points.shape[1] * cols * rows
    points = col_points.shape[1] * cols
    me = jnp.stack([lax.axis_index("col"), lax.axis_index("row")]).astype(jnp.int32)

    copies = jnp.broadcast_to(slab_points[None], (cols,) + slab_points.shape)
    slab = lax.all_to_all(copies, "col", 0, 0)

    order = [(k, flip) for flip in (0, 1) for k in range(cols // 2)]

    count = cols // 2
    half = count // 2
    strides = [stride for stride in halvings(cols) if stride > 1]
    own = col_points.shape[1] // rows
    part, first_kept, *prepared = first_sample_call(
        [(k, 1) for k in range(count)], me, slab, col_points, probes, own
    )
    got = exchanged(part, "col", 1)
    low, low_kept = next_sample_call([(k, 0) for k in range(half)], me, slab, *prepared[1:], own, part)
    low = low + got[:half]
    made, high_kept = next_sample_call(
        [(k, 0) for k in range(half, count)], me, slab, *prepared[1:], own, low
    )
    high = made + got[half:]
    kept = [low_kept, high_kept, first_kept]

    slabs = [later_call(slab, made)]
    for stride in halvings(rows):
        joined = slabs[0] if len(slabs) == 1 else jnp.concatenate(slabs, axis=0)
        slabs = [joined, exchanged(joined, "row", stride)]
    near = slabs[0].shape[0] // 2
    tiles = []
    spans = [(slabs[0], near), (slabs[1], 0), (slabs[1], near)]
    if rows > 4:
        spans = [(slabs[0], 0)] + spans
    for source, first in spans:
        chunks = [(base, k, flip) for base in range(first, first + near, cols) for k, flip in order]
        tiles.append(tile_call(me, source, chunks, prepared[0], own))
    tokens = [token for _, token in tiles]
    tiles = [tile for tile, _ in tiles]
    if rows > 4:
        tokens = [tokens[-1]] * 4

    for stride in strides:
        low = low + exchanged(low, "col", stride)
    for i, stride in enumerate(strides):
        high = sum_call(high, exchanged(high, "col", stride), *(tokens[:1] if i == 1 else []))
    sample = join_call(low, high)
    sample = join_call(sample, exchanged(sample, "col", 1), tokens[1])
    own_row = sample
    pieces = [sample]
    grams = []
    raws = []
    for stride in halvings(rows):
        if len(pieces) == 1:
            pieces.append(exchanged(pieces[0], "row", stride))
            continue
        wait = ()
        if stride == 1:
            gram, raw = partial_call(pieces[0], kept if rows == 4 else tiles[:1], own, rows == 4)
            grams.append(gram)
            raws.append(raw)
            wait = (gram, tokens[2])
        joined = join_call(*pieces, *wait)
        last = pieces[1]
        pieces = [joined, exchanged(joined, "row", stride)]
    gram, raw = partial_call(last, tiles[-3:-2], own)
    return tuple(
        finish_call(me, pieces[1], own_row, grams + [gram], raws + [raw], tiles[-2:], total, points)
    )


def solution(mesh):
    return jax.shard_map(
        body,
        mesh=mesh,
        in_specs=(P(None, ("row", "col")), P(None, "col"), P(None, "col")),
        out_specs=(P(None, ("row", "col")), P(None, ("col", "row"))),
        check_vma=False,
    )
```

```python
import functools

import jax
import jax.numpy as jnp
from jax import lax
from jax.experimental import pallas as pl
from jax.experimental.pallas import tpu as pltpu
from jax.sharding import PartitionSpec as P

MIB = 1024 * 1024


def params(mib):
    return pltpu.CompilerParams(vmem_limit_bytes=mib * MIB)


def split(x, pieces):
    out = []
    for _ in range(pieces):
        piece = x.astype(jnp.bfloat16)
        x = x - piece.astype(jnp.float32)
        out.append(piece)
    return out


def extended(points, scale=None):
    dims, count = points.shape
    wide = points.astype(jnp.float32)
    norm = -0.5 * jnp.sum(wide * wide, axis=0, keepdims=True)
    row = lax.broadcasted_iota(jnp.int32, (128 - dims, count), 0)
    at = 3 if scale is None else 0
    ones = 3 - at
    factor = 1.0 if scale is None else scale
    extra = jnp.where((row >= ones) & (row < ones + 3), factor, 0.0)
    for i, piece in enumerate(split(norm, 3)):
        extra = jnp.where(row == at + i, piece.astype(jnp.float32) * factor, extra)
    if scale is not None:
        points = (wide * scale).astype(jnp.bfloat16)
    return jnp.concatenate([points, extra.astype(jnp.bfloat16)], axis=0)


def chunks_of(*refs):
    return [ref[i] for ref in refs for i in range(ref.shape[0])]


def resident(shape, dtype):
    return pltpu.VMEM(shape, dtype)


def held(x):
    return pltpu.with_memory_space_constraint(x, pltpu.VMEM)


def pinned(x):
    return pltpu.with_memory_space_constraint(x, pltpu.HBM)


WHOLE = pl.BlockSpec(memory_space=pltpu.VMEM)
SCALAR = pl.BlockSpec(memory_space=pltpu.SMEM)


def add_sample(slab_ext, cols, probes, total, kept_ref, first, mine):
    step = min(256, total.shape[1])
    group = 2048
    own = kept_ref.shape[0] - 256
    places = []
    for j in range(cols.shape[0] // 256):
        place = first + j * 256 - mine
        place = jnp.where((place >= 0) & (place < own), place, own)
        places.append(pl.ds(pl.multiple_of(place, 256), 256))
    for i in range(total.shape[1] // step):
        at = slice(i * step, (i + 1) * step)
        slab = slab_ext[:, at]
        for g in range(cols.shape[0] // group):
            kernel = []
            for j in range(g * group // 256, (g + 1) * group // 256):
                rows = slice(j * 256, (j + 1) * 256)
                x = jnp.dot(cols[rows, :], slab, preferred_element_type=jnp.float32)
                k = jnp.exp(x).astype(jnp.bfloat16)
                kept_ref[places[j], at] = k
                kernel.append(k)
            total[:, at] += jnp.dot(
                probes[:, g * group : (g + 1) * group],
                jnp.concatenate(kernel, axis=0),
                preferred_element_type=jnp.float32,
            )


def start_sample(chunks, me_ref, slab_ref, slab_ext, total):
    side = me_ref[0] & 1
    points = [slab_ref[2 * k + (side ^ flip)] for k, flip in chunks]
    slab_ext[...] = extended(jnp.concatenate(points, axis=1), scale_of(slab_ref))
    total[...] = jnp.zeros_like(total)


def scale_of(slab_ref):
    return 16.0 / slab_ref.shape[1]


def end_sample(total, out_ref):
    share = out_ref.shape[2]
    for i in range(out_ref.shape[0]):
        out_ref[i] = total[:, i * share : (i + 1) * share]


def first_sample_kernel(chunks, me_ref, slab_ref, cols_ref, probes_ref, out_ref, kept_ref, cols_out,
                        turned_out, probes_out, slab_ext, total):
    step = pl.program_id(0)
    width = cols_ref.shape[1]

    @pl.when(step == 0)
    def _():
        start_sample(chunks, me_ref, slab_ref, slab_ext, total)

    at = pl.ds(pl.multiple_of(step * width, width), width)
    cols = extended(cols_ref[...])
    probes = probes_ref[...]
    turned = cols.T
    cols_out[:, at] = cols
    turned_out[at, :] = turned
    probes_out[:, at] = probes
    mine = me_ref[1] * (kept_ref.shape[0] - 256)
    add_sample(slab_ext, turned, probes, total, kept_ref, step * width, mine)

    @pl.when(step == pl.num_programs(0) - 1)
    def _():
        end_sample(total, out_ref)


def next_sample_kernel(chunks, me_ref, slab_ref, cols_ref, probes_ref, _, out_ref, kept_ref, slab_ext,
                       total):
    start_sample(chunks, me_ref, slab_ref, slab_ext, total)
    width = 8192
    mine = me_ref[1] * (kept_ref.shape[0] - 256)

    @pl.loop(0, cols_ref.shape[0] // width)
    def _(step):
        at = pl.ds(pl.multiple_of(step * width, width), width)
        add_sample(slab_ext, cols_ref[at, :], probes_ref[:, at], total, kept_ref, step * width, mine)

    end_sample(total, out_ref)


def sample_scratch(chunks, share, n):
    count = len(chunks) * share
    return [pltpu.VMEM((128, count), jnp.bfloat16), pltpu.VMEM((n, count), jnp.float32)]


def sample_cost(count, points):
    return pl.CostEstimate(
        flops=4 * 256 * count * points, bytes_accessed=512 * points, transcendentals=count * points
    )


def first_sample_call(chunks, me, slab, cols, probes, own):
    _, dims, share = slab.shape
    n, points = probes.shape
    width = 4096
    return pl.pallas_call(
        functools.partial(first_sample_kernel, chunks),
        grid=(points // width,),
        in_specs=[
            SCALAR,
            WHOLE,
            pl.BlockSpec((dims, width), lambda i: (0, i)),
            pl.BlockSpec((n, width), lambda i: (0, i)),
        ],
        out_specs=[WHOLE] * 5,
        out_shape=[
            jax.ShapeDtypeStruct((len(chunks), n, share), jnp.float32),
            resident((own + 256, len(chunks) * share), jnp.bfloat16),
            resident((128, points), jnp.bfloat16),
            resident((points, 128), jnp.bfloat16),
            resident((n, points), jnp.bfloat16),
        ],
        scratch_shapes=sample_scratch(chunks, share, n),
        compiler_params=params(10),
        cost_estimate=sample_cost(len(chunks) * share, points),
        name="sample_first",
    )(me, slab, pinned(cols), pinned(probes))


def next_sample_call(chunks, me, slab, cols_ext, probes, own, after):
    _, dims, share = slab.shape
    n, points = probes.shape
    return pl.pallas_call(
        functools.partial(next_sample_kernel, chunks),
        in_specs=[SCALAR] + [WHOLE] * 4,
        out_specs=[WHOLE] * 2,
        out_shape=[
            jax.ShapeDtypeStruct((len(chunks), n, share), jnp.float32),
            resident((own + 256, len(chunks) * share), jnp.bfloat16),
        ],
        scratch_shapes=sample_scratch(chunks, share, n),
        compiler_params=params(8),
        cost_estimate=sample_cost(len(chunks) * share, points),
        name="sample_next",
    )(me, slab, held(cols_ext), held(probes), after)


def tile_kernel(chunks, me_ref, slab_ref, cols_ref, out_ref, token_ref, slab_ext):
    token_ref[...] = jnp.zeros_like(token_ref)
    count, wide = out_ref.shape
    side = me_ref[0] & 1
    points = [slab_ref[base + 2 * k + (side ^ flip)] for base, k, flip in chunks]
    slab_ext[...] = extended(jnp.concatenate(points, axis=1), scale_of(slab_ref)).T
    mine = me_ref[1] * wide
    width = min(4096, wide)

    @pl.loop(0, wide // width)
    def _(step):
        for j in range(width // 256):
            to = pl.multiple_of(step * width + j * 256, 256)
            cols = cols_ref[:, pl.ds(pl.multiple_of(mine + to, 256), 256)]
            for i in range(count // 512):
                rows = slice(i * 512, (i + 1) * 512)
                x = jnp.dot(slab_ext[rows, :], cols, preferred_element_type=jnp.float32)
                out_ref[rows, pl.ds(to, 256)] = jnp.exp(x).astype(jnp.bfloat16)


def tile_call(me, slab, chunks, cols_ext, wide):
    dims, share = slab.shape[1:]
    count = len(chunks) * share
    return pl.pallas_call(
        functools.partial(tile_kernel, chunks),
        in_specs=[SCALAR, WHOLE, WHOLE],
        out_specs=[WHOLE, WHOLE],
        out_shape=[
            resident((count, wide), jnp.bfloat16),
            jax.ShapeDtypeStruct((8, 128), jnp.float32),
        ],
        scratch_shapes=[pltpu.VMEM((count, 128), jnp.bfloat16)],
        compiler_params=params(6 + count // 1024),
        cost_estimate=pl.CostEstimate(
            flops=2 * 256 * count * wide,
            bytes_accessed=2 * count * wide,
            transcendentals=count * wide,
        ),
        name="tile",
    )(me, slab, held(cols_ext))


def sum_kernel(a_ref, b_ref, *refs):
    refs[-1][...] = a_ref[...] + b_ref[...]


def sum_call(a, b, *after):
    return pl.pallas_call(
        sum_kernel,
        in_specs=[WHOLE] * (2 + len(after)),
        out_specs=WHOLE,
        out_shape=jax.ShapeDtypeStruct(a.shape, a.dtype),
        compiler_params=params(8),
        name="sum",
    )(a, b, *after)


def later_kernel(x_ref, _, out_ref):
    out_ref[...] = x_ref[...]


def later_call(x, after):
    return pl.pallas_call(
        later_kernel,
        in_specs=[WHOLE] * 2,
        out_specs=WHOLE,
        out_shape=jax.ShapeDtypeStruct(x.shape, x.dtype),
        compiler_params=params(8),
        name="later",
    )(x, after)


def join_kernel(a_ref, b_ref, *refs):
    out_ref = refs[-1]
    half = a_ref.shape[0]
    out_ref[:half] = a_ref[...]
    out_ref[half:] = b_ref[...]


def join_call(a, b, *after):
    return pl.pallas_call(
        join_kernel,
        in_specs=[WHOLE] * (2 + len(after)),
        out_specs=WHOLE,
        out_shape=jax.ShapeDtypeStruct((2 * a.shape[0],) + a.shape[1:], a.dtype),
        compiler_params=params(8),
        name="join",
    )(a, b, *after)


def inverse_factor(gram):
    n = gram.shape[0]
    depth = 8
    high = 8
    shape = (high, 2 * n)
    diagonal = lax.broadcasted_iota(jnp.int32, (n, n), 0) == lax.broadcasted_iota(jnp.int32, (n, n), 1)
    work = jnp.concatenate([gram, jnp.where(diagonal, 1.0, 0.0)], axis=1)
    blocks = [work[i : i + high, :] for i in range(0, n, high)]
    row = lax.broadcasted_iota(jnp.int32, shape, 0)

    def spread(x):
        return jnp.broadcast_to(x, shape)

    for first in range(0, n, depth):
        home, at = divmod(first, high)
        columns = [
            [spread(block[:, first + i : first + i + 1]) for i in range(depth)] for block in blocks[home:]
        ]
        lines = [spread(blocks[home][at + i : at + i + 1, :]) for i in range(depth)]
        entry = {
            (i, j): spread(columns[0][j][at + i : at + i + 1, :])
            for i in range(depth)
            for j in range(i + 1)
        }
        roots = []
        for j in range(depth):
            root = lax.rsqrt(entry[j, j])
            roots.append(root)
            inverse = root * root
            for i in range(j + 1, depth):
                factor = entry[i, j] * inverse
                for k in range(j + 1, i + 1):
                    entry[i, k] = entry[i, k] - factor * entry[k, j]
                lines[i] = lines[i] - factor * lines[j]
                for column in columns:
                    column[i] = column[i] - factor * column[j]
        scaled = [line * root for line, root in zip(lines, roots)]
        for b, column in enumerate(columns):
            block = blocks[home + b]
            update = (column[0] * roots[0]) * scaled[0]
            for i in range(1, depth):
                update = update + (column[i] * roots[i]) * scaled[i]
            if b:
                block = block - update
            else:
                block = jnp.where(row >= at + depth, block - update, block)
                for i in range(depth):
                    block = jnp.where(row == at + i, scaled[i], block)
            blocks[home + b] = block
        yield None
    yield jnp.concatenate(blocks, axis=0)[:, n:]


def sides(ref, turned):
    n, share = ref.shape[1:]
    for i, chunk in enumerate(chunks_of(ref)):
        turned[:, i * share : (i + 1) * share] = jnp.concatenate(split(chunk, 3), axis=0)
    pieces = turned[...]
    whole = lax.dot_general(
        pieces, pieces, (((1,), (1,)), ((), ())), preferred_element_type=jnp.float32
    )
    lines = whole[:n] + whole[n : 2 * n] + whole[2 * n :]
    return lines[:, :n] + lines[:, n : 2 * n] + lines[:, 2 * n :]


def product(turned, tiles, at, n, columns_first=False):
    first = 0
    lines = None
    for tile in tiles:
        last = first + tile.shape[1 if columns_first else 0]
        part = lax.dot_general(
            turned[: 2 * n, first:last],
            tile[at, :] if columns_first else tile[:, at],
            (((1,), (1 if columns_first else 0,)), ((), ())),
            preferred_element_type=jnp.float32,
        )
        lines = part if lines is None else lines + part
        first = last
    return lines[:n] + lines[n:]


def side_scratch(count, n):
    return [pltpu.VMEM((3 * n, count), jnp.bfloat16)]


def partial_kernel(columns_first, sample_ref, *refs):
    *tiles, gram_ref, raw_ref, turned = refs
    n = sample_ref.shape[1]
    gram_ref[...] = sides(sample_ref, turned)
    width = 512
    for i in range(raw_ref.shape[1] // width):
        at = slice(i * width, (i + 1) * width)
        raw_ref[:, at] = product(turned, tiles, at, n, columns_first)


def partial_call(sample, tiles, wide, columns_first=False):
    parts, n, share = sample.shape
    count = parts * share
    return pl.pallas_call(
        functools.partial(partial_kernel, columns_first),
        in_specs=[WHOLE] * (1 + len(tiles)),
        out_specs=[WHOLE, WHOLE],
        out_shape=[
            jax.ShapeDtypeStruct((n, n), jnp.float32),
            jax.ShapeDtypeStruct((n, wide), jnp.float32),
        ],
        scratch_shapes=side_scratch(count, n),
        compiler_params=params(6 + count // 1024),
        cost_estimate=pl.CostEstimate(
            flops=2 * 256 * count * wide, bytes_accessed=2 * count * wide, transcendentals=0
        ),
        name="partial",
    )(sample, *[held(tile) for tile in tiles])


def finish_kernel(total, points, me_ref, sample_ref, near_ref, gram_a, gram_b, raw_a, raw_b, c_ref, d_ref,
                  basis_ref, image_ref, turned, raw, left):
    n = sample_ref.shape[1]
    step = pl.program_id(0)
    half, wide = c_ref.shape

    @pl.when(step == 0)
    def _():
        gram = (sides(sample_ref, turned) + gram_a[...] + gram_b[...]) / total
        rounds = inverse_factor(gram)
        width = wide // 8
        for i in range(8):
            rows = slice(i * width, (i + 1) * width)
            for _ in range(n // 64):
                next(rounds)
            raw[:, rows] = product(turned, (c_ref, d_ref), rows, n) + (raw_a[:, rows] + raw_b[:, rows])
        inverse = next(rounds)
        while inverse is None:
            inverse = next(rounds)
        diagonal = (
            lax.broadcasted_iota(jnp.int32, (n, n), 0) == lax.broadcasted_iota(jnp.int32, (n, n), 1)
        )
        trace = jnp.sum(jnp.where(diagonal, gram, 0.0), keepdims=True)
        scale = jnp.sqrt(float(n * points) / trace) / total
        basis_ref[...] = jnp.dot(
            inverse,
            near_ref[me_ref[0] // 2],
            precision=lax.Precision.HIGHEST,
            preferred_element_type=jnp.float32,
        ).astype(jnp.bfloat16)
        high, low = split(inverse * scale, 2)
        left[...] = jnp.concatenate([high, high, low, low], axis=1)

    @pl.when(step > 0)
    def _():
        width = image_ref.shape[1]
        at = pl.ds(pl.multiple_of((step - 1) * width, width), width)
        pieces = split(raw[:, at], 2)
        image_ref[...] = jnp.dot(
            left[...], jnp.concatenate(pieces + pieces, axis=0), preferred_element_type=jnp.float32
        )


def finish_call(me, sample, near, grams, raws, tiles, total, points):
    _, n, share = sample.shape
    half, wide = tiles[0].shape
    count = 2 * half
    width = wide // 2
    return pl.pallas_call(
        functools.partial(finish_kernel, float(total), float(points)),
        grid=(3,),
        in_specs=[SCALAR] + [WHOLE] * 8,
        out_specs=[
            pl.BlockSpec((n, share), lambda i: (0, 0)),
            pl.BlockSpec((n, width), lambda i: (0, jnp.maximum(i - 1, 0))),
        ],
        out_shape=[
            jax.ShapeDtypeStruct((n, share), jnp.bfloat16),
            jax.ShapeDtypeStruct((n, wide), jnp.float32),
        ],
        scratch_shapes=side_scratch(count, n)
        + [pltpu.VMEM((n, wide), jnp.float32), pltpu.VMEM((n, 4 * n), jnp.bfloat16)],
        compiler_params=params(8 + count // 1024),
        cost_estimate=pl.CostEstimate(
            flops=2 * 256 * count * wide, bytes_accessed=2 * count * wide, transcendentals=0
        ),
        name="finish",
    )(me, sample, near, *grams, *raws, held(tiles[0]), held(tiles[1]))


def exchanged(x, axis, stride):
    return lax.ppermute(x, axis, [(i ^ stride, i) for i in range(lax.axis_size(axis))])


def halvings(size):
    while size > 1:
        size //= 2
        yield size


def body(slab_points, col_points, probes):
    cols = lax.axis_size("col")
    rows = lax.axis_size("row")
    total = slab_points.shape[1] * cols * rows
    points = col_points.shape[1] * cols
    me = jnp.stack([lax.axis_index("col"), lax.axis_index("row")]).astype(jnp.int32)

    copies = jnp.broadcast_to(slab_points[None], (cols,) + slab_points.shape)
    slab = lax.all_to_all(copies, "col", 0, 0)

    order = [(k, flip) for flip in (0, 1) for k in range(cols // 2)]

    count = cols // 2
    half = count // 2
    strides = [stride for stride in halvings(cols) if stride > 1]
    own = col_points.shape[1] // rows
    part, first_kept, *prepared = first_sample_call(
        [(k, 1) for k in range(count)], me, slab, col_points, probes, own
    )
    got = exchanged(part, "col", 1)
    low, low_kept = next_sample_call([(k, 0) for k in range(half)], me, slab, *prepared[1:], own, part)
    low = low + got[:half]
    made, high_kept = next_sample_call(
        [(k, 0) for k in range(half, count)], me, slab, *prepared[1:], own, low
    )
    high = made + got[half:]
    kept = [low_kept, high_kept, first_kept]

    slabs = [later_call(slab, made)]
    for stride in halvings(rows):
        joined = slabs[0] if len(slabs) == 1 else jnp.concatenate(slabs, axis=0)
        slabs = [joined, exchanged(joined, "row", stride)]
    near = slabs[0].shape[0] // 2
    tiles = []
    spans = [(slabs[0], near), (slabs[1], 0), (slabs[1], near)]
    if rows > 4:
        spans = [(slabs[0], 0)] + spans
    for source, first in spans:
        chunks = [(base, k, flip) for base in range(first, first + near, cols) for k, flip in order]
        tiles.append(tile_call(me, source, chunks, prepared[0], own))
    tokens = [token for _, token in tiles]
    tiles = [tile for tile, _ in tiles]
    if rows > 4:
        tokens = [tokens[-1]] * 4

    for stride in strides:
        low = low + exchanged(low, "col", stride)
    for i, stride in enumerate(strides):
        high = sum_call(high, exchanged(high, "col", stride), *(tokens[:1] if i == 1 else []))
    sample = join_call(low, high)
    sample = join_call(sample, exchanged(sample, "col", 1), tokens[1])
    own_row = sample
    pieces = [sample]
    grams = []
    raws = []
    for stride in halvings(rows):
        if len(pieces) == 1:
            pieces.append(exchanged(pieces[0], "row", stride))
            continue
        wait = ()
        if stride == 1:
            gram, raw = partial_call(pieces[0], kept if rows == 4 else tiles[:1], own, rows == 4)
            grams.append(gram)
            raws.append(raw)
            wait = (gram, tokens[2])
        joined = join_call(*pieces, *wait)
        last = pieces[1]
        pieces = [joined, exchanged(joined, "row", stride)]
    gram, raw = partial_call(last, tiles[-3:-2], own)
    return tuple(
        finish_call(me, pieces[1], own_row, grams + [gram], raws + [raw], tiles[-2:], total, points)
    )


def solution(mesh):
    return jax.shard_map(
        body,
        mesh=mesh,
        in_specs=(P(None, ("row", "col")), P(None, "col"), P(None, "col")),
        out_specs=(P(None, ("row", "col")), P(None, ("col", "row"))),
        check_vma=False,
    )
```

```python
import functools

import jax
import jax.numpy as jnp
from jax import lax
from jax.experimental import pallas as pl
from jax.experimental.pallas import tpu as pltpu
from jax.sharding import PartitionSpec as P

MIB = 1024 * 1024


def params(mib):
    return pltpu.CompilerParams(vmem_limit_bytes=mib * MIB)


def split(x, pieces):
    out = []
    for _ in range(pieces):
        piece = x.astype(jnp.bfloat16)
        x = x - piece.astype(jnp.float32)
        out.append(piece)
    return out


def extended(points, scale=None):
    dims, count = points.shape
    wide = points.astype(jnp.float32)
    norm = -0.5 * jnp.sum(wide * wide, axis=0, keepdims=True)
    row = lax.broadcasted_iota(jnp.int32, (128 - dims, count), 0)
    at = 3 if scale is None else 0
    ones = 3 - at
    factor = 1.0 if scale is None else scale
    extra = jnp.where((row >= ones) & (row < ones + 3), factor, 0.0)
    for i, piece in enumerate(split(norm, 3)):
        extra = jnp.where(row == at + i, piece.astype(jnp.float32) * factor, extra)
    if scale is not None:
        points = (wide * scale).astype(jnp.bfloat16)
    return jnp.concatenate([points, extra.astype(jnp.bfloat16)], axis=0)


def chunks_of(*refs):
    return [ref[i] for ref in refs for i in range(ref.shape[0])]


def resident(shape, dtype):
    return pltpu.VMEM(shape, dtype)


def held(x):
    return pltpu.with_memory_space_constraint(x, pltpu.VMEM)


def pinned(x):
    return pltpu.with_memory_space_constraint(x, pltpu.HBM)


WHOLE = pl.BlockSpec(memory_space=pltpu.VMEM)
SCALAR = pl.BlockSpec(memory_space=pltpu.SMEM)


def add_sample(slab_ext, cols, probes, total, kept_ref, first, mine):
    step = min(256, total.shape[1])
    group = 2048
    own = kept_ref.shape[0] - 256
    places = []
    for j in range(cols.shape[0] // 256):
        place = first + j * 256 - mine
        place = jnp.where((place >= 0) & (place < own), place, own)
        places.append(pl.ds(pl.multiple_of(place, 256), 256))
    for i in range(total.shape[1] // step):
        at = slice(i * step, (i + 1) * step)
        slab = slab_ext[:, at]
        for g in range(cols.shape[0] // group):
            kernel = []
            for j in range(g * group // 256, (g + 1) * group // 256):
                rows = slice(j * 256, (j + 1) * 256)
                x = jnp.dot(cols[rows, :], slab, preferred_element_type=jnp.float32)
                k = jnp.exp(x).astype(jnp.bfloat16)
                kept_ref[places[j], at] = k
                kernel.append(k)
            total[:, at] += jnp.dot(
                probes[:, g * group : (g + 1) * group],
                jnp.concatenate(kernel, axis=0),
                preferred_element_type=jnp.float32,
            )


def start_sample(chunks, me_ref, slab_ref, slab_ext, total):
    side = me_ref[0] & 1
    points = [slab_ref[2 * k + (side ^ flip)] for k, flip in chunks]
    slab_ext[...] = extended(jnp.concatenate(points, axis=1), scale_of(slab_ref))
    total[...] = jnp.zeros_like(total)


def scale_of(slab_ref):
    return 16.0 / slab_ref.shape[1]


def end_sample(total, out_ref):
    share = out_ref.shape[2]
    for i in range(out_ref.shape[0]):
        out_ref[i] = total[:, i * share : (i + 1) * share]


def first_sample_kernel(chunks, me_ref, slab_ref, cols_ref, probes_ref, out_ref, kept_ref, cols_out,
                        turned_out, probes_out, slab_ext, total):
    step = pl.program_id(0)
    width = cols_ref.shape[1]

    @pl.when(step == 0)
    def _():
        start_sample(chunks, me_ref, slab_ref, slab_ext, total)

    at = pl.ds(pl.multiple_of(step * width, width), width)
    cols = extended(cols_ref[...])
    probes = probes_ref[...]
    turned = cols.T
    cols_out[:, at] = cols
    turned_out[at, :] = turned
    probes_out[:, at] = probes
    mine = me_ref[1] * (kept_ref.shape[0] - 256)
    add_sample(slab_ext, turned, probes, total, kept_ref, step * width, mine)

    @pl.when(step == pl.num_programs(0) - 1)
    def _():
        end_sample(total, out_ref)


def next_sample_kernel(chunks, me_ref, slab_ref, cols_ref, probes_ref, _, out_ref, kept_ref, slab_ext,
                       total):
    start_sample(chunks, me_ref, slab_ref, slab_ext, total)
    width = 8192
    mine = me_ref[1] * (kept_ref.shape[0] - 256)

    @pl.loop(0, cols_ref.shape[0] // width)
    def _(step):
        at = pl.ds(pl.multiple_of(step * width, width), width)
        add_sample(slab_ext, cols_ref[at, :], probes_ref[:, at], total, kept_ref, step * width, mine)

    end_sample(total, out_ref)


def sample_scratch(chunks, share, n):
    count = len(chunks) * share
    return [pltpu.VMEM((128, count), jnp.bfloat16), pltpu.VMEM((n, count), jnp.float32)]


def sample_cost(count, points):
    return pl.CostEstimate(
        flops=4 * 256 * count * points, bytes_accessed=512 * points, transcendentals=count * points
    )


def first_sample_call(chunks, me, slab, cols, probes, own):
    _, dims, share = slab.shape
    n, points = probes.shape
    width = 4096
    return pl.pallas_call(
        functools.partial(first_sample_kernel, chunks),
        grid=(points // width,),
        in_specs=[
            SCALAR,
            WHOLE,
            pl.BlockSpec((dims, width), lambda i: (0, i)),
            pl.BlockSpec((n, width), lambda i: (0, i)),
        ],
        out_specs=[WHOLE] * 5,
        out_shape=[
            jax.ShapeDtypeStruct((len(chunks), n, share), jnp.float32),
            resident((own + 256, len(chunks) * share), jnp.bfloat16),
            resident((128, points), jnp.bfloat16),
            resident((points, 128), jnp.bfloat16),
            resident((n, points), jnp.bfloat16),
        ],
        scratch_shapes=sample_scratch(chunks, share, n),
        compiler_params=params(10),
        cost_estimate=sample_cost(len(chunks) * share, points),
        name="sample_first",
    )(me, slab, pinned(cols), pinned(probes))


def next_sample_call(chunks, me, slab, cols_ext, probes, own, after):
    _, dims, share = slab.shape
    n, points = probes.shape
    return pl.pallas_call(
        functools.partial(next_sample_kernel, chunks),
        in_specs=[SCALAR] + [WHOLE] * 4,
        out_specs=[WHOLE] * 2,
        out_shape=[
            jax.ShapeDtypeStruct((len(chunks), n, share), jnp.float32),
            resident((own + 256, len(chunks) * share), jnp.bfloat16),
        ],
        scratch_shapes=sample_scratch(chunks, share, n),
        compiler_params=params(8),
        cost_estimate=sample_cost(len(chunks) * share, points),
        name="sample_next",
    )(me, slab, held(cols_ext), held(probes), after)


def tile_kernel(chunks, me_ref, slab_ref, cols_ref, out_ref, token_ref, slab_ext):
    token_ref[...] = jnp.zeros_like(token_ref)
    count, wide = out_ref.shape
    side = me_ref[0] & 1
    points = [slab_ref[base + 2 * k + (side ^ flip)] for base, k, flip in chunks]
    slab_ext[...] = extended(jnp.concatenate(points, axis=1), scale_of(slab_ref)).T
    mine = me_ref[1] * wide
    width = min(4096, wide)

    @pl.loop(0, wide // width)
    def _(step):
        for j in range(width // 256):
            to = pl.multiple_of(step * width + j * 256, 256)
            cols = cols_ref[:, pl.ds(pl.multiple_of(mine + to, 256), 256)]
            for i in range(count // 512):
                rows = slice(i * 512, (i + 1) * 512)
                x = jnp.dot(slab_ext[rows, :], cols, preferred_element_type=jnp.float32)
                out_ref[rows, pl.ds(to, 256)] = jnp.exp(x).astype(jnp.bfloat16)


def tile_call(me, slab, chunks, cols_ext, wide):
    dims, share = slab.shape[1:]
    count = len(chunks) * share
    return pl.pallas_call(
        functools.partial(tile_kernel, chunks),
        in_specs=[SCALAR, WHOLE, WHOLE],
        out_specs=[WHOLE, WHOLE],
        out_shape=[
            resident((count, wide), jnp.bfloat16),
            jax.ShapeDtypeStruct((8, 128), jnp.float32),
        ],
        scratch_shapes=[pltpu.VMEM((count, 128), jnp.bfloat16)],
        compiler_params=params(6 + count // 1024),
        cost_estimate=pl.CostEstimate(
            flops=2 * 256 * count * wide,
            bytes_accessed=2 * count * wide,
            transcendentals=count * wide,
        ),
        name="tile",
    )(me, slab, held(cols_ext))


def sum_kernel(a_ref, b_ref, *refs):
    refs[-1][...] = a_ref[...] + b_ref[...]


def sum_call(a, b, *after):
    return pl.pallas_call(
        sum_kernel,
        in_specs=[WHOLE] * (2 + len(after)),
        out_specs=WHOLE,
        out_shape=jax.ShapeDtypeStruct(a.shape, a.dtype),
        compiler_params=params(8),
        name="sum",
    )(a, b, *after)


def later_kernel(x_ref, _, out_ref):
    out_ref[...] = x_ref[...]


def later_call(x, after):
    return pl.pallas_call(
        later_kernel,
        in_specs=[WHOLE] * 2,
        out_specs=WHOLE,
        out_shape=jax.ShapeDtypeStruct(x.shape, x.dtype),
        compiler_params=params(8),
        name="later",
    )(x, after)


def join_kernel(a_ref, b_ref, *refs):
    out_ref = refs[-1]
    half = a_ref.shape[0]
    out_ref[:half] = a_ref[...]
    out_ref[half:] = b_ref[...]


def join_call(a, b, *after):
    return pl.pallas_call(
        join_kernel,
        in_specs=[WHOLE] * (2 + len(after)),
        out_specs=WHOLE,
        out_shape=jax.ShapeDtypeStruct((2 * a.shape[0],) + a.shape[1:], a.dtype),
        compiler_params=params(8),
        name="join",
    )(a, b, *after)


def inverse_factor(gram):
    n = gram.shape[0]
    depth = 8
    high = 8
    shape = (high, 2 * n)
    diagonal = lax.broadcasted_iota(jnp.int32, (n, n), 0) == lax.broadcasted_iota(jnp.int32, (n, n), 1)
    work = jnp.concatenate([gram, jnp.where(diagonal, 1.0, 0.0)], axis=1)
    blocks = [work[i : i + high, :] for i in range(0, n, high)]
    row = lax.broadcasted_iota(jnp.int32, shape, 0)

    def spread(x):
        return jnp.broadcast_to(x, shape)

    for first in range(0, n, depth):
        home, at = divmod(first, high)
        columns = [
            [spread(block[:, first + i : first + i + 1]) for i in range(depth)] for block in blocks[home:]
        ]
        lines = [spread(blocks[home][at + i : at + i + 1, :]) for i in range(depth)]
        entry = {
            (i, j): spread(columns[0][j][at + i : at + i + 1, :])
            for i in range(depth)
            for j in range(i + 1)
        }
        roots = []
        for j in range(depth):
            root = lax.rsqrt(entry[j, j])
            roots.append(root)
            inverse = root * root
            for i in range(j + 1, depth):
                factor = entry[i, j] * inverse
                for k in range(j + 1, i + 1):
                    entry[i, k] = entry[i, k] - factor * entry[k, j]
                lines[i] = lines[i] - factor * lines[j]
                for column in columns:
                    column[i] = column[i] - factor * column[j]
        scaled = [line * root for line, root in zip(lines, roots)]
        for b, column in enumerate(columns):
            block = blocks[home + b]
            update = (column[0] * roots[0]) * scaled[0]
            for i in range(1, depth):
                update = update + (column[i] * roots[i]) * scaled[i]
            if b:
                block = block - update
            else:
                block = jnp.where(row >= at + depth, block - update, block)
                for i in range(depth):
                    block = jnp.where(row == at + i, scaled[i], block)
            blocks[home + b] = block
        yield None
    yield jnp.concatenate(blocks, axis=0)[:, n:]


def sides(ref, turned):
    n, share = ref.shape[1:]
    for i, chunk in enumerate(chunks_of(ref)):
        turned[:, i * share : (i + 1) * share] = jnp.concatenate(split(chunk, 3), axis=0)
    pieces = turned[...]
    whole = lax.dot_general(
        pieces, pieces, (((1,), (1,)), ((), ())), preferred_element_type=jnp.float32
    )
    lines = whole[:n] + whole[n : 2 * n] + whole[2 * n :]
    return lines[:, :n] + lines[:, n : 2 * n] + lines[:, 2 * n :]


def product(turned, tiles, at, n, columns_first=False):
    first = 0
    lines = None
    for tile in tiles:
        last = first + tile.shape[1 if columns_first else 0]
        part = lax.dot_general(
            turned[: 2 * n, first:last],
            tile[at, :] if columns_first else tile[:, at],
            (((1,), (1 if columns_first else 0,)), ((), ())),
            preferred_element_type=jnp.float32,
        )
        lines = part if lines is None else lines + part
        first = last
    return lines[:n] + lines[n:]


def side_scratch(count, n):
    return [pltpu.VMEM((3 * n, count), jnp.bfloat16)]


def partial_kernel(columns_first, sample_ref, *refs):
    *tiles, gram_ref, raw_ref, turned = refs
    n = sample_ref.shape[1]
    gram_ref[...] = sides(sample_ref, turned)
    width = 512
    for i in range(raw_ref.shape[1] // width):
        at = slice(i * width, (i + 1) * width)
        raw_ref[:, at] = product(turned, tiles, at, n, columns_first)


def partial_call(sample, tiles, wide, columns_first=False):
    parts, n, share = sample.shape
    count = parts * share
    return pl.pallas_call(
        functools.partial(partial_kernel, columns_first),
        in_specs=[WHOLE] * (1 + len(tiles)),
        out_specs=[WHOLE, WHOLE],
        out_shape=[
            jax.ShapeDtypeStruct((n, n), jnp.float32),
            jax.ShapeDtypeStruct((n, wide), jnp.float32),
        ],
        scratch_shapes=side_scratch(count, n),
        compiler_params=params(6 + count // 1024),
        cost_estimate=pl.CostEstimate(
            flops=2 * 256 * count * wide, bytes_accessed=2 * count * wide, transcendentals=0
        ),
        name="partial",
    )(sample, *[held(tile) for tile in tiles])


def finish_kernel(total, points, me_ref, sample_ref, near_ref, gram_a, gram_b, raw_a, raw_b, c_ref, d_ref,
                  basis_ref, image_ref, turned, raw, left):
    n = sample_ref.shape[1]
    step = pl.program_id(0)
    half, wide = c_ref.shape

    @pl.when(step == 0)
    def _():
        gram = (sides(sample_ref, turned) + gram_a[...] + gram_b[...]) / total
        rounds = inverse_factor(gram)
        width = wide // 8
        for i in range(8):
            rows = slice(i * width, (i + 1) * width)
            if i < 4:
                next(rounds)
                next(rounds)
            raw[:, rows] = product(turned, (c_ref, d_ref), rows, n) + (raw_a[:, rows] + raw_b[:, rows])
        inverse = next(rounds)
        while inverse is None:
            inverse = next(rounds)
        diagonal = (
            lax.broadcasted_iota(jnp.int32, (n, n), 0) == lax.broadcasted_iota(jnp.int32, (n, n), 1)
        )
        trace = jnp.sum(jnp.where(diagonal, gram, 0.0), keepdims=True)
        scale = jnp.sqrt(float(n * points) / trace) / total
        basis_ref[...] = jnp.dot(
            inverse,
            near_ref[me_ref[0] // 2],
            precision=lax.Precision.HIGHEST,
            preferred_element_type=jnp.float32,
        ).astype(jnp.bfloat16)
        high, low = split(inverse * scale, 2)
        left[...] = jnp.concatenate([high, high, low, low], axis=1)

    @pl.when(step > 0)
    def _():
        width = image_ref.shape[1]
        at = pl.ds(pl.multiple_of((step - 1) * width, width), width)
        pieces = split(raw[:, at], 2)
        image_ref[...] = jnp.dot(
            left[...], jnp.concatenate(pieces + pieces, axis=0), preferred_element_type=jnp.float32
        )


def finish_call(me, sample, near, grams, raws, tiles, total, points):
    _, n, share = sample.shape
    half, wide = tiles[0].shape
    count = 2 * half
    width = wide
    return pl.pallas_call(
        functools.partial(finish_kernel, float(total), float(points)),
        grid=(2,),
        in_specs=[SCALAR] + [WHOLE] * 8,
        out_specs=[
            pl.BlockSpec((n, share), lambda i: (0, 0)),
            pl.BlockSpec((n, width), lambda i: (0, jnp.maximum(i - 1, 0))),
        ],
        out_shape=[
            jax.ShapeDtypeStruct((n, share), jnp.bfloat16),
            jax.ShapeDtypeStruct((n, wide), jnp.float32),
        ],
        scratch_shapes=side_scratch(count, n)
        + [pltpu.VMEM((n, wide), jnp.float32), pltpu.VMEM((n, 4 * n), jnp.bfloat16)],
        compiler_params=params(10 + count // 1024),
        cost_estimate=pl.CostEstimate(
            flops=2 * 256 * count * wide, bytes_accessed=2 * count * wide, transcendentals=0
        ),
        name="finish",
    )(me, sample, near, *grams, *raws, held(tiles[0]), held(tiles[1]))


def exchanged(x, axis, stride):
    return lax.ppermute(x, axis, [(i ^ stride, i) for i in range(lax.axis_size(axis))])


def halvings(size):
    while size > 1:
        size //= 2
        yield size


def body(slab_points, col_points, probes):
    cols = lax.axis_size("col")
    rows = lax.axis_size("row")
    total = slab_points.shape[1] * cols * rows
    points = col_points.shape[1] * cols
    me = jnp.stack([lax.axis_index("col"), lax.axis_index("row")]).astype(jnp.int32)

    copies = jnp.broadcast_to(slab_points[None], (cols,) + slab_points.shape)
    slab = lax.all_to_all(copies, "col", 0, 0)

    order = [(k, flip) for flip in (0, 1) for k in range(cols // 2)]

    count = cols // 2
    half = count // 2
    strides = [stride for stride in halvings(cols) if stride > 1]
    own = col_points.shape[1] // rows
    part, first_kept, *prepared = first_sample_call(
        [(k, 1) for k in range(count)], me, slab, col_points, probes, own
    )
    got = exchanged(part, "col", 1)
    low, low_kept = next_sample_call([(k, 0) for k in range(half)], me, slab, *prepared[1:], own, part)
    low = low + got[:half]
    made, high_kept = next_sample_call(
        [(k, 0) for k in range(half, count)], me, slab, *prepared[1:], own, low
    )
    high = made + got[half:]
    kept = [low_kept, high_kept, first_kept]

    slabs = [later_call(slab, made)]
    for stride in halvings(rows):
        joined = slabs[0] if len(slabs) == 1 else jnp.concatenate(slabs, axis=0)
        slabs = [joined, exchanged(joined, "row", stride)]
    near = slabs[0].shape[0] // 2
    tiles = []
    spans = [(slabs[0], near), (slabs[1], 0), (slabs[1], near)]
    if rows > 4:
        spans = [(slabs[0], 0)] + spans
    for source, first in spans:
        chunks = [(base, k, flip) for base in range(first, first + near, cols) for k, flip in order]
        tiles.append(tile_call(me, source, chunks, prepared[0], own))
    tokens = [token for _, token in tiles]
    tiles = [tile for tile, _ in tiles]
    if rows > 4:
        tokens = [tokens[-1]] * 4

    for stride in strides:
        low = low + exchanged(low, "col", stride)
    for i, stride in enumerate(strides):
        high = sum_call(high, exchanged(high, "col", stride), *(tokens[:1] if i == 1 else []))
    sample = join_call(low, high)
    sample = join_call(sample, exchanged(sample, "col", 1), tokens[1])
    own_row = sample
    pieces = [sample]
    grams = []
    raws = []
    for stride in halvings(rows):
        if len(pieces) == 1:
            pieces.append(exchanged(pieces[0], "row", stride))
            continue
        wait = ()
        if stride == 1:
            gram, raw = partial_call(pieces[0], kept if rows == 4 else tiles[:1], own, rows == 4)
            grams.append(gram)
            raws.append(raw)
            wait = (gram, tokens[2])
        joined = join_call(*pieces, *wait)
        last = pieces[1]
        pieces = [joined, exchanged(joined, "row", stride)]
    gram, raw = partial_call(last, tiles[-3:-2], own)
    return tuple(
        finish_call(me, pieces[1], own_row, grams + [gram], raws + [raw], tiles[-2:], total, points)
    )


def solution(mesh):
    return jax.shard_map(
        body,
        mesh=mesh,
        in_specs=(P(None, ("row", "col")), P(None, "col"), P(None, "col")),
        out_specs=(P(None, ("row", "col")), P(None, ("col", "row"))),
        check_vma=False,
    )
```
